32 devices in a mesh: leaf: 16 (over z, x, core), seq: 2 (over y).
Axes of the slice: x: 2, y: 2, z: 4, core: 2. Of those that a mesh axis runs over, the one named last changes fastest.
Arguments:
- queries: bfloat16 [16, 128, 8192], P('leaf', 'seq'), may hold values from -120 to 120
- leaf_kv: bfloat16 [16, 128, 2048], P('leaf', 'seq'), may hold values from -144 to 144
- cache: bfloat16 [2048, 2048], P(('leaf', 'seq')), may hold values from -144 to 144
- out_weight: bfloat16 [8192, 5120], P(None, 'seq'), may hold values from -0.0625 to 0.0625
- parent: int32 [26], replicated, may hold values from 0 to 9, as said below
- owner: int32 [10], replicated, may hold values from 0 to 15, as said below
- lengths: int32 [10], replicated, may hold values from 32 to 128, as said below
Outputs:
- projected: bfloat16 [16, 128, 5120], P('leaf', None, 'seq')
The draws below stay inside these ranges and needn't reach their ends.
Inputs may be any that keep to these rules, and one draw needn't show every extreme that they name: Entries 0 to 9 are segments: segment i < 4 has parent i - 1 (segment 0 has 0), the next 2 have parent 4 - 1, the next 4 each a segment of those 2; entries 10 on are the leaves, each with a parent among the last 4 segments. `owner`: distinct slots. `lengths`: some segment has exactly 128.
All inputs are finite; a program needn't handle non-finite values.
Results may differ from the reference program's by a relative error of at most 0.012.
Values may be sent and summed in bfloat16 or wider, within the bound.
A program may use at most 256 MiB of HBM per device.

```python
import math
import jax
import jax.numpy as jnp
from jax import lax

D = 5120
KVH = 8
GROUP = 8
HD = 128
CAP = 128
PCH = 4
LEAF_LEN = 128
B1 = 2
B2 = 4
SEGS = 10
DEPTH = 6
N_LEAF = 16


def leaf_keys(key):
    return jnp.clip(jax.random.normal(key, (N_LEAF, LEAF_LEN, KVH, HD), jnp.float32), -6.0, 6.0)


def draw_queries(key, part):
    key = jax.random.fold_in(key, 11)
    normal_rows = jnp.clip(jax.random.normal(key, (N_LEAF, LEAF_LEN, KVH * GROUP * HD), jnp.float32), -6.0, 6.0)
    result = normal_rows
    return result.astype(jnp.bfloat16)


def draw_leaf_kv(key, part):
    base = leaf_keys(key).reshape(N_LEAF, LEAF_LEN, KVH * HD)
    key = jax.random.fold_in(key, 3)
    value_key = jax.random.fold_in(key, 1)
    keys_part = base
    values_part = 24.0 * jnp.clip(jax.random.normal(value_key, base.shape, jnp.float32), -6.0, 6.0)
    return jnp.concatenate([keys_part, values_part], axis=2).astype(jnp.bfloat16)


def draw_cache(key, part):
    key = jax.random.fold_in(key, 5)
    key_key, value_key = jax.random.split(key)
    keys_part = jnp.clip(jax.random.normal(key_key, (N_LEAF * CAP, KVH * HD), jnp.float32), -6.0, 6.0)
    values_part = 24.0 * jnp.clip(jax.random.normal(value_key, (N_LEAF * CAP, KVH * HD), jnp.float32), -6.0, 6.0)
    return jnp.concatenate([keys_part, values_part], axis=1).astype(jnp.bfloat16)


def draw_parent(key, part):
    key = jax.random.fold_in(key, 7)
    key_one, key_two, key_three, key_four = jax.random.split(key, 4)
    prompt_part = jnp.maximum(jnp.arange(PCH, dtype=jnp.int32) - 1, 0)
    first_level = jnp.full((B1,), PCH - 1, jnp.int32)
    second_pick = jnp.concatenate([jnp.arange(B1, dtype=jnp.int32), jax.random.randint(key_one, (B2 - B1,), 0, B1, jnp.int32)])
    second_level = second_pick[jax.random.permutation(key_two, B2)] + PCH
    leaf_pick = jnp.concatenate([jnp.arange(B2, dtype=jnp.int32), jax.random.randint(key_three, (N_LEAF - B2,), 0, B2, jnp.int32)])
    leaf_level = leaf_pick[jax.random.permutation(key_four, N_LEAF)] + PCH + B1
    return jnp.concatenate([prompt_part, first_level, second_level, leaf_level]).astype(jnp.int32)


def draw_owner(key, part):
    key = jax.random.fold_in(key, 13)
    return jax.random.permutation(key, N_LEAF)[:SEGS].astype(jnp.int32)


def draw_lengths(key, part):
    key = jax.random.fold_in(key, 17)
    key_one, key_two = jax.random.split(key)
    drawn = jax.random.randint(key_one, (SEGS,), CAP // 4, CAP + 1, jnp.int32)
    chosen = jax.random.randint(key_two, (), 0, SEGS, jnp.int32)
    return drawn.at[chosen].set(CAP).astype(jnp.int32)


def block_scale(own_key, dims, cuts, low, high):
    def one(axis_at, blocks):
        draws = jax.random.uniform(jax.random.fold_in(jax.random.fold_in(own_key, 6), axis_at), (blocks,), jnp.float32, low / len(cuts), high / len(cuts))
        return jnp.repeat(jnp.exp(draws), dims[axis_at] // blocks).reshape((-1,) + (1,) * (len(dims) - axis_at - 1))

    factor_of = one(*cuts[0])
    for cut in cuts[1:]:
        factor_of = factor_of * one(*cut)
    return factor_of


def noise(own_key, dims, deviation, limit, shards=(), kind=jnp.bfloat16):
    level = block_scale(own_key, dims, shards, -0.22, 0.18) if shards else 1.0
    values = jax.random.normal(own_key, dims, jnp.float32) * deviation * level
    return jnp.minimum(jnp.maximum(values, -limit), limit).astype(kind)


def setup_inputs(seed: int = 0) -> dict:
    key_list = jax.random.split(jax.random.key(seed), 8)
    queries = draw_queries(jax.random.fold_in(key_list[7], 71), 0)
    leaf_kv = draw_leaf_kv(jax.random.fold_in(key_list[7], 71), 0)
    cache = draw_cache(jax.random.fold_in(key_list[7], 71), 0)
    out_weight = noise(key_list[3], (KVH * GROUP * HD, D), (KVH * GROUP * HD) ** -0.5, 0.0625, ((1, 2),))
    parent = draw_parent(jax.random.fold_in(key_list[7], 71), 0)
    owner = draw_owner(jax.random.fold_in(key_list[7], 71), 0)
    lengths = draw_lengths(jax.random.fold_in(key_list[7], 71), 0)
    return dict(queries=queries, leaf_kv=leaf_kv, cache=cache, out_weight=out_weight, parent=parent, owner=owner, lengths=lengths)


def branch(parent, leaf_index, seg_count):
    segment = parent[seg_count + leaf_index]
    ancestry = [segment]
    for level in range(DEPTH - 1):
        segment = parent[segment]
        ancestry.append(segment)
    return jnp.stack(ancestry).astype(jnp.int32)

def reference(queries, leaf_kv, cache, out_weight, parent, owner, lengths):
    slot_cache = cache.reshape(N_LEAF, CAP, 2 * KVH * HD)
    block_rows = math.gcd(LEAF_LEN, 256)
    blocks = LEAF_LEN // block_rows
    score_scale = 1.0 / math.sqrt(HD)

    def one_leaf(leaf_index):
        ancestry = branch(parent, leaf_index, SEGS)
        branch_rows = slot_cache[owner[ancestry]].reshape(DEPTH * CAP, 2 * KVH * HD)
        branch_usable = (jnp.arange(CAP)[None, :] < lengths[ancestry][:, None]).reshape(-1)
        key_value = jnp.concatenate([branch_rows, leaf_kv[leaf_index]], axis=0).astype(jnp.float32)
        keys_all = key_value[:, :KVH * HD].reshape(-1, KVH, HD)
        values_all = key_value[:, KVH * HD:].reshape(-1, KVH, HD)
        query_rows = queries[leaf_index].reshape(blocks, block_rows, KVH, GROUP, HD)
        positions = jnp.arange(LEAF_LEN).reshape(blocks, block_rows)

        def one_block(operands):
            query_block, position = operands
            scores = jnp.einsum('qhgd,khd->qhgk', query_block.astype(jnp.float32), keys_all) * score_scale
            leaf_usable = jnp.arange(LEAF_LEN)[None, :] <= position[:, None]
            usable = jnp.concatenate([jnp.broadcast_to(branch_usable[None, :], (block_rows, DEPTH * CAP)), leaf_usable], axis=1)
            scores = jnp.where(usable[:, None, None, :], scores, -jnp.inf)
            largest = lax.optimization_barrier(jnp.max(scores, axis=3, keepdims=True))
            expon = jnp.exp(scores - largest)
            total = lax.optimization_barrier(jnp.sum(expon, axis=3))
            weights = lax.optimization_barrier(expon.astype(jnp.bfloat16))
            summed = jnp.einsum('qhgk,khd->qhgd', weights.astype(jnp.float32), values_all)
            attended = (summed / total[:, :, :, None]).astype(jnp.bfloat16)
            return attended.reshape(block_rows, KVH * GROUP * HD)
        attended = lax.map(one_block, (query_rows, positions)).reshape(LEAF_LEN, KVH * GROUP * HD)
        return jnp.dot(attended, out_weight, preferred_element_type=jnp.float32).astype(jnp.bfloat16)
    return lax.map(one_leaf, jnp.arange(N_LEAF, dtype=jnp.int32))
```

```python
import functools
import math

import jax
import jax.numpy as jnp
from jax import lax
from jax.experimental import pallas as pl
from jax.experimental.pallas import tpu as pltpu
from jax.sharding import PartitionSpec as P

KVH = 8
GROUP = 8
HD = 128
DEPTH = 6
WSLOTS = 4
NEG = -1e30
MESH = pl.DeviceIdType.MESH


def kernel(
    n_leaf, n_seq, cap,
    q_hbm, leaf_hbm, cache_hbm, w_hbm, parent, owner, lengths,
    out,
    kvb, qb, lb, wb, kcat, vcat, att, acc, bias,
    local_sem, w_sem, y_send, y_recv, ring_send, ring_recv, sib_send, sib_recv,
):
    chips = n_leaf // 2
    half = chips // 2
    tokens = q_hbm.shape[1]
    rows = cache_hbm.shape[0]
    all_tokens = n_seq * tokens
    cols = w_hbm.shape[1]
    me = lax.axis_index("leaf")
    seq = lax.axis_index("seq")
    core = lax.rem(me, 2)
    chip = me // 2
    side = lax.rem(chip, 2)
    level = chip // 2
    pos = level * (1 - side) + (chips - 1 - level) * side

    def slot_at(place, which):
        place = lax.rem(place + 2 * chips, chips)
        far = place // half
        return 2 * (2 * (place * (1 - far) + (chips - 1 - place) * far) + far) + which

    right = slot_at(pos + 1, core)
    left = slot_at(pos - 1, core)
    sibling = 2 * chip + 1 - core
    peers = [lax.rem(seq + d, n_seq) for d in range(1, n_seq)]

    def own(c):
        k_cols = pl.ds(pl.multiple_of(c * HD, HD), HD)
        v_cols = pl.ds(pl.multiple_of((KVH + c) * HD, HD), HD)
        q_cols = pl.ds(pl.multiple_of(c * GROUP * HD, HD), GROUP * HD)
        pairs = (
            (cache_hbm.at[:, k_cols], kvb.at[c, me, seq, 0]),
            (cache_hbm.at[:, v_cols], kvb.at[c, me, seq, 1]),
            (leaf_hbm.at[0, :, k_cols], lb.at[c, seq, 0]),
            (leaf_hbm.at[0, :, v_cols], lb.at[c, seq, 1]),
            (q_hbm.at[0, :, q_cols], qb.at[c, seq]),
        )
        return [
            pltpu.make_async_copy(src, dst, local_sem.at[c, i])
            for i, (src, dst) in enumerate(pairs)
        ]

    def weight(c):
        slot = lax.rem(c, WSLOTS)
        k = GROUP * HD
        return pltpu.make_async_copy(
            w_hbm.at[pl.ds(pl.multiple_of(c * k, k), k), :], wb.at[slot], w_sem.at[slot]
        )

    def remote(ref, send, recv, leaf, s):
        return pltpu.make_async_remote_copy(
            src_ref=ref, dst_ref=ref, send_sem=send, recv_sem=recv,
            device_id=(leaf, s), device_id_type=MESH,
        )

    def across(c, d, kind, at, to):
        ref = (kvb.at[c, me, at], lb.at[c, at], qb.at[c, at])[kind]
        return remote(ref, y_send.at[c, d, kind], y_recv.at[c, d, kind], me, to)

    def across_out(c, d, kind):
        return across(c, d, kind, seq, peers[d])

    def across_in(c, d, kind):
        return across(c, d, kind, lax.rem(seq + n_seq - d - 1, n_seq), peers[d])

    def block(c, slot, step, way):
        if step < half:
            return kvb.at[c, slot]
        return kvb.at[c, slot, pl.ds(way * (n_seq // 2), n_seq // 2)]

    def ring_out(c, step, way):
        place = pos - (step - 1) if way == 0 else pos + (step - 1)
        ref = block(c, slot_at(place, core), step, way)
        i = 2 * (step - 1) + way
        return remote(ref, ring_send.at[c, i], ring_recv.at[c, i], (right, left)[way], seq)

    def ring_in(c, step, way):
        place = pos - step if way == 0 else pos + step
        ref = block(c, slot_at(place, core), step, way)
        i = 2 * (step - 1) + way
        return remote(ref, ring_send.at[c, i], ring_recv.at[c, i], (left, right)[way], seq)

    def share(c, step, way, which):
        place = pos - step if way == 0 else pos + step
        ref = block(c, slot_at(place, which), step, way)
        i = 0 if step == 0 else 1 + 2 * (step - 1) + way
        return remote(ref, sib_send.at[c, i], sib_recv.at[c, i], sibling, seq)

    hops = [(step, way) for step in range(1, half + 1) for way in range(2)]

    @pl.loop(0, KVH)
    def _(c):
        for copy in own(c):
            copy.start()

    for c in range(WSLOTS):
        weight(c).start()

    barrier = pltpu.get_barrier_semaphore()
    partners = [(right, seq), (left, seq), (sibling, seq)] + [(me, p) for p in peers]
    for partner in partners:
        pl.semaphore_signal(barrier, inc=1, device_id=partner, device_id_type=MESH)
    pl.semaphore_wait(barrier, len(partners))

    segment = parent[owner.shape[0] + me]
    slots = []
    for a in range(DEPTH):
        slots.append(owner[segment])
        lane = lax.broadcasted_iota(jnp.int32, (8, cap), 1)
        bias[:, a * cap:(a + 1) * cap] = jnp.where(lane < lengths[segment], 0.0, NEG)
        segment = parent[segment]
    acc[...] = jnp.zeros_like(acc)

    stack = max(1, 256 // all_tokens)
    branch_keys = DEPTH * cap
    factor = math.log2(math.e) / math.sqrt(HD)

    def select(c):
        for j in range(n_seq):
            for part, cat in ((0, kcat), (1, vcat)):
                def pick(s, found):
                    piece = kvb[c, s, j, part]
                    return tuple(
                        lax.select(slots[a] == s, piece, found[a]) for a in range(DEPTH)
                    )
                zero = jnp.zeros((rows, HD), jnp.bfloat16)
                found = lax.fori_loop(0, n_leaf, pick, (zero,) * DEPTH)
                for a in range(DEPTH):
                    cat[a * cap + j * rows:a * cap + (j + 1) * rows, :] = found[a]
                at = branch_keys + j * tokens
                cat[at:at + tokens, :] = lb[c, j, part]

    def attend(c):
        def heads(i, carry):
            parts = []
            for g in range(stack):
                lanes = pl.ds(pl.multiple_of((i * stack + g) * HD, HD), HD)
                for j in range(n_seq):
                    parts.append(qb[c, j, :, lanes])
            q = jnp.concatenate(parts, axis=0)
            dims = (((1,), (1,)), ((), ()))
            scores = lax.dot_general(q, kcat[...], dims, preferred_element_type=jnp.float32)
            seen = scores[:, :branch_keys] + bias[0:1, :]
            count = stack * all_tokens
            row = lax.broadcasted_iota(jnp.int32, (count, all_tokens), 0)
            key = lax.broadcasted_iota(jnp.int32, (count, all_tokens), 1)
            own_keys = jnp.where(key <= lax.rem(row, all_tokens), scores[:, branch_keys:], NEG)
            scores = jnp.concatenate([seen, own_keys], axis=1)
            largest = jnp.max(scores, axis=1, keepdims=True)
            expon = jnp.exp2((scores - largest) * factor)
            total = jnp.sum(expon, axis=1, keepdims=True)
            summed = jnp.dot(
                expon.astype(jnp.bfloat16), vcat[...], preferred_element_type=jnp.float32
            )
            result = (summed / total).astype(jnp.bfloat16)
            for g in range(stack):
                lanes = pl.ds(pl.multiple_of((i * stack + g) * HD, HD), HD)
                att[:, lanes] = result[g * all_tokens:(g + 1) * all_tokens]
            return carry
        lax.fori_loop(0, GROUP // stack, heads, 0)

    tile = math.gcd(cols, 512)

    def project(c):
        slot = lax.rem(c, WSLOTS)
        @pl.loop(0, cols // tile)
        def _(i):
            at = pl.ds(pl.multiple_of(i * tile, tile), tile)
            acc[:, at] += jnp.dot(att[...], wb[slot, :, at], preferred_element_type=jnp.float32)

    last = half + 2

    @pl.loop(0, KVH + last)
    def _(tick):
        def when(offset):
            c = tick - offset
            return c, pl.when((c >= 0) & (c < KVH))

        for step in range(half + 1, 0, -1):
            c, guard = when(step)

            @guard
            def _(c=c, step=step):
                if step == 1:
                    for d in range(n_seq - 1):
                        across_in(c, d, 0).wait_recv()
                    for way in range(2):
                        ring_out(c, 1, way).start()
                    share(c, 0, 0, core).start()
                else:
                    for way in range(2):
                        ring_in(c, step - 1, way).wait_recv()
                        if step <= half:
                            ring_out(c, step, way).start()
                        share(c, step - 1, way, core).start()

        c, guard = when(0)

        @guard
        def _(c=c):
            for copy in own(c):
                copy.wait()
            for kind in range(3):
                for d in range(n_seq - 1):
                    across_out(c, d, kind).start()

        c, guard = when(last)

        @guard
        def _(c=c):
            for step, way in [(0, 0)] + hops:
                share(c, step, way, 1 - core).wait_recv()
            for d in range(n_seq - 1):
                across_in(c, d, 1).wait_recv()
                across_in(c, d, 2).wait_recv()
            select(c)
            attend(c)
            weight(c).wait()
            project(c)

            @pl.when(c + WSLOTS < KVH)
            def _():
                weight(c + WSLOTS).start()

    out[0] = acc[...].astype(out.dtype)

    @pl.loop(0, KVH)
    def _(c):
        for kind in range(3):
            for d in range(n_seq - 1):
                across_out(c, d, kind).wait_send()
        for step, way in hops:
            ring_out(c, step, way).wait_send()
        for step, way in [(0, 0)] + hops:
            share(c, step, way, core).wait_send()


def per_device(n_leaf, n_seq, queries, leaf_kv, cache, out_weight, parent, owner, lengths):
    tokens = queries.shape[1]
    rows = cache.shape[0]
    cap = rows * n_seq
    total = tokens * n_seq
    cols = out_weight.shape[1]
    hops = n_leaf // 2
    hbm = pl.BlockSpec(memory_space=pl.ANY)
    smem = pl.BlockSpec(memory_space=pltpu.SMEM)
    keys = DEPTH * cap + total
    dma = pltpu.SemaphoreType.DMA
    bf16 = jnp.bfloat16
    return pl.pallas_call(
        functools.partial(kernel, n_leaf, n_seq, cap),
        out_shape=jax.ShapeDtypeStruct((1, total, cols), bf16),
        in_specs=[hbm] * 4 + [smem] * 3,
        out_specs=pl.BlockSpec(memory_space=pltpu.VMEM),
        scratch_shapes=[
            pltpu.VMEM((KVH, n_leaf, n_seq, 2, rows, HD), bf16),
            pltpu.VMEM((KVH, n_seq, tokens, GROUP * HD), bf16),
            pltpu.VMEM((KVH, n_seq, 2, tokens, HD), bf16),
            pltpu.VMEM((WSLOTS, GROUP * HD, cols), bf16),
            pltpu.VMEM((keys, HD), bf16),
            pltpu.VMEM((keys, HD), bf16),
            pltpu.VMEM((total, GROUP * HD), bf16),
            pltpu.VMEM((total, cols), jnp.float32),
            pltpu.VMEM((8, DEPTH * cap), jnp.float32),
            dma((KVH, 5)),
            dma((WSLOTS,)),
            dma((KVH, n_seq - 1, 3)),
            dma((KVH, n_seq - 1, 3)),
            dma((KVH, hops)),
            dma((KVH, hops)),
            dma((KVH, hops + 1)),
            dma((KVH, hops + 1)),
        ],
        compiler_params=pltpu.CompilerParams(
            collective_id=0, has_side_effects=True, vmem_limit_bytes=58 * 1024 * 1024
        ),
    )(queries, leaf_kv, cache, out_weight, parent, owner, lengths)


def solution(mesh):
    in_specs = (
        P("leaf", "seq", None),
        P("leaf", "seq", None),
        P(("leaf", "seq"), None),
        P(None, "seq"),
        P(),
        P(),
        P(),
    )
    out_specs = P("leaf", None, "seq")
    return jax.shard_map(
        functools.partial(per_device, mesh.shape["leaf"], mesh.shape["seq"]),
        mesh=mesh, in_specs=in_specs, out_specs=out_specs, check_vma=False,
    )
```

```python
import functools
import math

import jax
import jax.numpy as jnp
from jax import lax
from jax.experimental import pallas as pl
from jax.experimental.pallas import tpu as pltpu
from jax.sharding import PartitionSpec as P

KVH = 8
GROUP = 8
HD = 128
DEPTH = 6
NEG = -1e30
MESH = pl.DeviceIdType.MESH


def kernel(
    n_leaf, n_seq, cap,
    q_hbm, leaf_hbm, cache_hbm, w_hbm, parent, owner, lengths,
    out,
    kvb, qb, lb, wb, kcat, vcat, att, acc, bias,
    local_sem, w_sem, y_send, y_recv, ring_send, ring_recv, sib_send, sib_recv,
    att_send, att_recv,
):
    chips = n_leaf // 2
    half = chips // 2
    tokens = q_hbm.shape[1]
    rows = cache_hbm.shape[0]
    all_tokens = n_seq * tokens
    cols = w_hbm.shape[1]
    me = lax.axis_index("leaf")
    seq = lax.axis_index("seq")
    core = lax.rem(me, 2)
    chip = me // 2
    side = lax.rem(chip, 2)
    level = chip // 2
    pos = level * (1 - side) + (chips - 1 - level) * side

    def slot_at(place, which):
        place = lax.rem(place + 2 * chips, chips)
        far = place // half
        return 2 * (2 * (place * (1 - far) + (chips - 1 - place) * far) + far) + which

    right = slot_at(pos + 1, core)
    left = slot_at(pos - 1, core)
    sibling = 2 * chip + 1 - core
    peers = [lax.rem(seq + d, n_seq) for d in range(1, n_seq)]

    share_heads = KVH // n_seq
    width = GROUP * HD

    def pieces(c, to):
        head = to * share_heads + c
        k_cols = pl.ds(pl.multiple_of(head * HD, HD), HD)
        v_cols = pl.ds(pl.multiple_of((KVH + head) * HD, HD), HD)
        q_cols = pl.ds(pl.multiple_of(head * width, width), width)
        return (
            cache_hbm.at[:, k_cols],
            cache_hbm.at[:, v_cols],
            leaf_hbm.at[0, :, k_cols],
            leaf_hbm.at[0, :, v_cols],
            q_hbm.at[0, :, q_cols],
        )

    def places(c, origin):
        return (
            kvb.at[c, me, origin, 0],
            kvb.at[c, me, origin, 1],
            lb.at[c, origin, 0],
            lb.at[c, origin, 1],
            qb.at[c, origin],
        )

    def own(c):
        return [
            pltpu.make_async_copy(src, dst, local_sem.at[c, i])
            for i, (src, dst) in enumerate(zip(pieces(c, seq), places(c, seq)))
        ]

    def weight(head):
        return pltpu.make_async_copy(
            w_hbm.at[pl.ds(pl.multiple_of(head * width, width), width), :],
            wb.at[head],
            w_sem.at[head],
        )

    def copy_to(src, dst, send, recv, leaf, s):
        return pltpu.make_async_remote_copy(
            src_ref=src, dst_ref=dst, send_sem=send, recv_sem=recv,
            device_id=(leaf, s), device_id_type=MESH,
        )

    def remote(ref, send, recv, leaf, s):
        return copy_to(ref, ref, send, recv, leaf, s)

    def source(d):
        return lax.rem(seq + n_seq - d - 1, n_seq)

    def across_out(c, d, kind):
        return copy_to(
            pieces(c, peers[d])[kind], places(c, seq)[kind],
            y_send.at[c, d, kind], y_recv.at[c, d, kind], me, peers[d],
        )

    def across_in(c, d, kind):
        ref = places(c, source(d))[kind]
        return remote(ref, y_send.at[c, d, kind], y_recv.at[c, d, kind], me, source(d))

    def attended(c, i, d, origin, to):
        ref = att.at[origin, c, i]
        return remote(ref, att_send.at[c, i, d], att_recv.at[c, i, d], me, to)

    def block(c, slot, step, way):
        if step < half:
            return kvb.at[c, slot]
        return kvb.at[c, slot, pl.ds(way * (n_seq // 2), n_seq // 2)]

    def ring_out(c, step, way):
        place = pos - (step - 1) if way == 0 else pos + (step - 1)
        ref = block(c, slot_at(place, core), step, way)
        i = 2 * (step - 1) + way
        return remote(ref, ring_send.at[c, i], ring_recv.at[c, i], (right, left)[way], seq)

    def ring_in(c, step, way):
        place = pos - step if way == 0 else pos + step
        ref = block(c, slot_at(place, core), step, way)
        i = 2 * (step - 1) + way
        return remote(ref, ring_send.at[c, i], ring_recv.at[c, i], (left, right)[way], seq)

    def share(c, step, way, which):
        place = pos - step if way == 0 else pos + step
        ref = block(c, slot_at(place, which), step, way)
        i = 0 if step == 0 else 1 + 2 * (step - 1) + way
        return remote(ref, sib_send.at[c, i], sib_recv.at[c, i], sibling, seq)

    hops = [(step, way) for step in range(1, half + 1) for way in range(2)]

    @pl.loop(0, share_heads)
    def _(c):
        for copy in own(c):
            copy.start()

    barrier = pltpu.get_barrier_semaphore()
    partners = [(right, seq), (left, seq), (sibling, seq)] + [(me, p) for p in peers]
    for partner in partners:
        pl.semaphore_signal(barrier, inc=1, device_id=partner, device_id_type=MESH)
    pl.semaphore_wait(barrier, len(partners))

    segment = parent[owner.shape[0] + me]
    slots = []
    for a in range(DEPTH):
        slots.append(owner[segment])
        lane = lax.broadcasted_iota(jnp.int32, (8, cap), 1)
        bias[:, a * cap:(a + 1) * cap] = jnp.where(lane < lengths[segment], 0.0, NEG)
        segment = parent[segment]
    acc[...] = jnp.zeros_like(acc)

    stack = max(1, 256 // all_tokens)
    branch_keys = DEPTH * cap
    factor = math.log2(math.e) / math.sqrt(HD)

    def select(c):
        for j in range(n_seq):
            for part, cat in ((0, kcat), (1, vcat)):
                def pick(s, found):
                    piece = kvb[c, s, j, part]
                    return tuple(
                        lax.select(slots[a] == s, piece, found[a]) for a in range(DEPTH)
                    )
                zero = jnp.zeros((rows, HD), jnp.bfloat16)
                found = lax.fori_loop(0, n_leaf, pick, (zero,) * DEPTH, unroll=4)
                for a in range(DEPTH):
                    cat[a * cap + j * rows:a * cap + (j + 1) * rows, :] = found[a]
                at = branch_keys + j * tokens
                cat[at:at + tokens, :] = lb[c, j, part]

    def stacked(c, first):
        parts = []
        for g in range(stack):
            lanes = pl.ds(pl.multiple_of((first + g) * HD, HD), HD)
            for j in range(n_seq):
                parts.append(qb[c, j, :, lanes])
        q = jnp.concatenate(parts, axis=0)
        dims = (((1,), (1,)), ((), ()))
        scores = lax.dot_general(q, kcat[...], dims, preferred_element_type=jnp.float32)
        seen = scores[:, :branch_keys] + bias[0:1, :]
        count = stack * all_tokens
        row = lax.broadcasted_iota(jnp.int32, (count, all_tokens), 0)
        key = lax.broadcasted_iota(jnp.int32, (count, all_tokens), 1)
        own_keys = jnp.where(key <= lax.rem(row, all_tokens), scores[:, branch_keys:], NEG)
        scores = jnp.concatenate([seen, own_keys], axis=1)
        largest = jnp.max(scores, axis=1, keepdims=True)
        expon = jnp.exp2((scores - largest) * factor)
        total = jnp.sum(expon, axis=1, keepdims=True)
        summed = jnp.dot(
            expon.astype(jnp.bfloat16), vcat[...], preferred_element_type=jnp.float32
        )
        result = (summed / total).astype(jnp.bfloat16)
        return [result[g * all_tokens:(g + 1) * all_tokens] for g in range(stack)]

    parts_per_head = att.shape[2]
    group = GROUP // parts_per_head

    def attend(c):
        @pl.loop(0, parts_per_head)
        def _(i):
            results = []
            for first in range(0, group, stack):
                results += stacked(c, i * group + first)
            att[seq, c, i] = jnp.concatenate(results, axis=1)
            for d in range(n_seq - 1):
                attended(c, i, d, seq, peers[d]).start()

    tile = math.gcd(cols, 512)

    def project(origin, c):
        head = origin * share_heads + c
        weight(head).wait()
        rows_in = jnp.concatenate(
            [att[origin, c, i] for i in range(parts_per_head)], axis=1
        )

        @pl.loop(0, cols // tile)
        def _(i):
            at = pl.ds(pl.multiple_of(i * tile, tile), tile)
            acc[:, at] += jnp.dot(rows_in, wb[head, :, at], preferred_element_type=jnp.float32)

    last = half + 2

    @pl.loop(0, max(KVH, share_heads + last + 1))
    def _(tick):
        def when(offset):
            c = tick - offset
            return c, pl.when((c >= 0) & (c < share_heads))

        for step in range(half + 1, 0, -1):
            c, guard = when(step)

            @guard
            def _(c=c, step=step):
                if step == 1:
                    for copy in own(c):
                        copy.wait()
                    for d in range(n_seq - 1):
                        across_in(c, d, 0).wait_recv()
                        across_in(c, d, 1).wait_recv()
                    for way in range(2):
                        ring_out(c, 1, way).start()
                    share(c, 0, 0, core).start()
                else:
                    for way in range(2):
                        ring_in(c, step - 1, way).wait_recv()
                        if step <= half:
                            ring_out(c, step, way).start()
                        share(c, step - 1, way, core).start()

        c, guard = when(0)

        @guard
        def _(c=c):
            for kind in range(5):
                for d in range(n_seq - 1):
                    across_out(c, d, kind).start()

        @pl.when(tick < KVH)
        def _():
            weight(lax.rem(seq * share_heads + tick, KVH)).start()

        c, guard = when(last)

        @guard
        def _(c=c):
            for step, way in [(0, 0)] + hops:
                share(c, step, way, 1 - core).wait_recv()
            for d in range(n_seq - 1):
                for kind in range(2, 5):
                    across_in(c, d, kind).wait_recv()
            select(c)
            attend(c)
            project(seq, c)

        c, guard = when(last + 1)

        @guard
        def _(c=c):
            for d in range(n_seq - 1):
                for i in range(parts_per_head):
                    attended(c, i, d, source(d), source(d)).wait_recv()
                project(source(d), c)

    out[0] = acc[...].astype(out.dtype)

    @pl.loop(0, share_heads)
    def _(c):
        for d in range(n_seq - 1):
            for kind in range(5):
                across_out(c, d, kind).wait_send()
            for i in range(parts_per_head):
                attended(c, i, d, seq, peers[d]).wait_send()
        for step, way in hops:
            ring_out(c, step, way).wait_send()
        for step, way in [(0, 0)] + hops:
            share(c, step, way, core).wait_send()


def per_device(n_leaf, n_seq, queries, leaf_kv, cache, out_weight, parent, owner, lengths):
    tokens = queries.shape[1]
    rows = cache.shape[0]
    cap = rows * n_seq
    total = tokens * n_seq
    cols = out_weight.shape[1]
    hops = n_leaf // 2
    heads = KVH // n_seq
    group = min(GROUP, 2 * max(1, 256 // total))
    parts = GROUP // group
    hbm = pl.BlockSpec(memory_space=pl.ANY)
    smem = pl.BlockSpec(memory_space=pltpu.SMEM)
    keys = DEPTH * cap + total
    dma = pltpu.SemaphoreType.DMA
    bf16 = jnp.bfloat16
    return pl.pallas_call(
        functools.partial(kernel, n_leaf, n_seq, cap),
        out_shape=jax.ShapeDtypeStruct((1, total, cols), bf16),
        in_specs=[hbm] * 4 + [smem] * 3,
        out_specs=pl.BlockSpec(memory_space=pltpu.VMEM),
        scratch_shapes=[
            pltpu.VMEM((heads, n_leaf, n_seq, 2, rows, HD), bf16),
            pltpu.VMEM((heads, n_seq, tokens, GROUP * HD), bf16),
            pltpu.VMEM((heads, n_seq, 2, tokens, HD), bf16),
            pltpu.VMEM((KVH, GROUP * HD, cols), bf16),
            pltpu.VMEM((keys, HD), bf16),
            pltpu.VMEM((keys, HD), bf16),
            pltpu.VMEM((n_seq, heads, parts, total, group * HD), bf16),
            pltpu.VMEM((total, cols), jnp.float32),
            pltpu.VMEM((8, DEPTH * cap), jnp.float32),
            dma((heads, 5)),
            dma((KVH,)),
            dma((heads, n_seq - 1, 5)),
            dma((heads, n_seq - 1, 5)),
            dma((heads, hops)),
            dma((heads, hops)),
            dma((heads, hops + 1)),
            dma((heads, hops + 1)),
            dma((heads, parts, n_seq - 1)),
            dma((heads, parts, n_seq - 1)),
        ],
        compiler_params=pltpu.CompilerParams(
            collective_id=0, has_side_effects=True, vmem_limit_bytes=58 * 1024 * 1024
        ),
    )(queries, leaf_kv, cache, out_weight, parent, owner, lengths)


def solution(mesh):
    in_specs = (
        P("leaf", "seq", None),
        P("leaf", "seq", None),
        P(("leaf", "seq"), None),
        P(None, "seq"),
        P(),
        P(),
        P(),
    )
    out_specs = P("leaf", None, "seq")
    return jax.shard_map(
        functools.partial(per_device, mesh.shape["leaf"], mesh.shape["seq"]),
        mesh=mesh, in_specs=in_specs, out_specs=out_specs, check_vma=False,
    )
```

```python
import functools
import math

import jax
import jax.numpy as jnp
from jax import lax
from jax.experimental import pallas as pl
from jax.experimental.pallas import tpu as pltpu
from jax.sharding import PartitionSpec as P

KVH = 8
GROUP = 8
HD = 128
DEPTH = 6
NEG = -1e30
MESH = pl.DeviceIdType.MESH


def kernel(
    n_leaf, n_seq, cap,
    q_hbm, leaf_hbm, cache_hbm, w_hbm, parent, owner, lengths,
    out,
    kvb, qb, lb, wb, kcat, vcat, att, acc, bias,
    local_sem, w_sem, y_send, y_recv, ring_send, ring_recv, sib_send, sib_recv,
    att_send, att_recv,
):
    chips = n_leaf // 2
    half = chips // 2
    tokens = q_hbm.shape[1]
    rows = cache_hbm.shape[0]
    all_tokens = n_seq * tokens
    cols = w_hbm.shape[1]
    me = lax.axis_index("leaf")
    seq = lax.axis_index("seq")
    core = lax.rem(me, 2)
    chip = me // 2
    side = lax.rem(chip, 2)
    level = chip // 2
    pos = level * (1 - side) + (chips - 1 - level) * side

    def slot_at(place, which):
        place = lax.rem(place + 2 * chips, chips)
        far = place // half
        return 2 * (2 * (place * (1 - far) + (chips - 1 - place) * far) + far) + which

    right = slot_at(pos + 1, core)
    left = slot_at(pos - 1, core)
    sibling = 2 * chip + 1 - core
    peers = [lax.rem(seq + d, n_seq) for d in range(1, n_seq)]

    share_heads = KVH // n_seq
    width = GROUP * HD

    def pieces(c, to):
        head = to * share_heads + c
        k_cols = pl.ds(pl.multiple_of(head * HD, HD), HD)
        v_cols = pl.ds(pl.multiple_of((KVH + head) * HD, HD), HD)
        q_cols = pl.ds(pl.multiple_of(head * width, width), width)
        return (
            cache_hbm.at[:, k_cols],
            cache_hbm.at[:, v_cols],
            leaf_hbm.at[0, :, k_cols],
            leaf_hbm.at[0, :, v_cols],
            q_hbm.at[0, :, q_cols],
        )

    def places(c, origin):
        return (
            kvb.at[c, me, origin, 0],
            kvb.at[c, me, origin, 1],
            lb.at[c, origin, 0],
            lb.at[c, origin, 1],
            qb.at[c, origin],
        )

    def own(c):
        return [
            pltpu.make_async_copy(src, dst, local_sem.at[c, i])
            for i, (src, dst) in enumerate(zip(pieces(c, seq), places(c, seq)))
        ]

    def weight(head):
        return pltpu.make_async_copy(
            w_hbm.at[pl.ds(pl.multiple_of(head * width, width), width), :],
            wb.at[head],
            w_sem.at[head],
        )

    def copy_to(src, dst, send, recv, leaf, s):
        return pltpu.make_async_remote_copy(
            src_ref=src, dst_ref=dst, send_sem=send, recv_sem=recv,
            device_id=(leaf, s), device_id_type=MESH,
        )

    def remote(ref, send, recv, leaf, s):
        return copy_to(ref, ref, send, recv, leaf, s)

    def source(d):
        return lax.rem(seq + n_seq - d - 1, n_seq)

    def across_out(c, d, kind):
        return copy_to(
            pieces(c, peers[d])[kind], places(c, seq)[kind],
            y_send.at[c, d, kind], y_recv.at[c, d, kind], me, peers[d],
        )

    def across_in(c, d, kind):
        ref = places(c, source(d))[kind]
        return remote(ref, y_send.at[c, d, kind], y_recv.at[c, d, kind], me, source(d))

    def attended(c, i, d, origin, to):
        ref = att.at[origin, c, i]
        return remote(ref, att_send.at[c, i, d], att_recv.at[c, i, d], me, to)

    def block(c, slot, step, way):
        if step < half:
            return kvb.at[c, slot]
        return kvb.at[c, slot, pl.ds(way * (n_seq // 2), n_seq // 2)]

    def ring_out(c, step, way):
        place = pos - (step - 1) if way == 0 else pos + (step - 1)
        ref = block(c, slot_at(place, core), step, way)
        i = 2 * (step - 1) + way
        return remote(ref, ring_send.at[c, i], ring_recv.at[c, i], (right, left)[way], seq)

    def ring_in(c, step, way):
        place = pos - step if way == 0 else pos + step
        ref = block(c, slot_at(place, core), step, way)
        i = 2 * (step - 1) + way
        return remote(ref, ring_send.at[c, i], ring_recv.at[c, i], (left, right)[way], seq)

    def share(c, step, way, which):
        place = pos - step if way == 0 else pos + step
        ref = block(c, slot_at(place, which), step, way)
        i = 0 if step == 0 else 1 + 2 * (step - 1) + way
        return remote(ref, sib_send.at[c, i], sib_recv.at[c, i], sibling, seq)

    hops = [(step, way) for step in range(1, half + 1) for way in range(2)]

    @pl.loop(0, share_heads)
    def _(c):
        for copy in own(c):
            copy.start()

    barrier = pltpu.get_barrier_semaphore()
    partners = [(right, seq), (left, seq), (sibling, seq)] + [(me, p) for p in peers]
    for partner in partners:
        pl.semaphore_signal(barrier, inc=1, device_id=partner, device_id_type=MESH)
    pl.semaphore_wait(barrier, len(partners))

    @pl.loop(0, share_heads)
    def _(c):
        for d in range(n_seq - 1):
            across_out(c, d, 0).start()
            across_out(c, d, 1).start()

    segment = parent[owner.shape[0] + me]
    slots = []
    for a in range(DEPTH):
        slots.append(owner[segment])
        lane = lax.broadcasted_iota(jnp.int32, (8, cap), 1)
        bias[:, a * cap:(a + 1) * cap] = jnp.where(lane < lengths[segment], 0.0, NEG)
        segment = parent[segment]

    stack = max(1, 256 // all_tokens)
    branch_keys = DEPTH * cap
    factor = math.log2(math.e) / math.sqrt(HD)

    def select(c):
        for j in range(n_seq):
            for part, cat in ((0, kcat), (1, vcat)):
                def pick(s, found):
                    piece = kvb[c, s, j, part]
                    return tuple(
                        lax.select(slots[a] == s, piece, found[a]) for a in range(DEPTH)
                    )
                zero = jnp.zeros((rows, HD), jnp.bfloat16)
                found = lax.fori_loop(0, n_leaf, pick, (zero,) * DEPTH, unroll=4)
                for a in range(DEPTH):
                    cat[a * cap + j * rows:a * cap + (j + 1) * rows, :] = found[a]
                at = branch_keys + j * tokens
                cat[at:at + tokens, :] = lb[c, j, part]

    def stacked(c, first):
        parts = []
        for g in range(stack):
            lanes = pl.ds(pl.multiple_of((first + g) * HD, HD), HD)
            for j in range(n_seq):
                parts.append(qb[c, j, :, lanes])
        q = jnp.concatenate(parts, axis=0)
        dims = (((1,), (1,)), ((), ()))
        scores = lax.dot_general(q, kcat[...], dims, preferred_element_type=jnp.float32)
        seen = scores[:, :branch_keys] + bias[0:1, :]
        count = stack * all_tokens
        row = lax.broadcasted_iota(jnp.int32, (count, all_tokens), 0)
        key = lax.broadcasted_iota(jnp.int32, (count, all_tokens), 1)
        own_keys = jnp.where(key <= lax.rem(row, all_tokens), scores[:, branch_keys:], NEG)
        scores = jnp.concatenate([seen, own_keys], axis=1)
        largest = jnp.max(scores, axis=1, keepdims=True)
        expon = jnp.exp2((scores - largest) * factor)
        total = jnp.sum(expon, axis=1, keepdims=True)
        summed = jnp.dot(
            expon.astype(jnp.bfloat16), vcat[...], preferred_element_type=jnp.float32
        )
        result = (summed / total).astype(jnp.bfloat16)
        return [result[g * all_tokens:(g + 1) * all_tokens] for g in range(stack)]

    parts_per_head = att.shape[2]
    group = GROUP // parts_per_head

    def attend(c):
        @pl.loop(0, parts_per_head)
        def _(i):
            results = []
            for first in range(0, group, stack):
                results += stacked(c, i * group + first)
            att[seq, c, i] = jnp.concatenate(results, axis=1)
            for d in range(n_seq - 1):
                attended(c, i, d, seq, peers[d]).start()

    tile = math.gcd(cols, 512)

    def rows_of(origin, c):
        return jnp.concatenate([att[origin, c, i] for i in range(parts_per_head)], axis=1)

    def product(origin, c, at):
        head = origin * share_heads + c
        return jnp.dot(rows_of(origin, c), wb[head, :, at], preferred_element_type=jnp.float32)

    def project_own():
        for c in range(share_heads):
            weight(seq * share_heads + c).wait()

        @pl.loop(0, cols // tile)
        def _(i):
            at = pl.ds(pl.multiple_of(i * tile, tile), tile)
            part = product(seq, 0, at)
            for c in range(1, share_heads):
                part += product(seq, c, at)
            acc[:, at] = part

    def project(origin, c):
        weight(origin * share_heads + c).wait()

        @pl.loop(0, cols // tile)
        def _(i):
            at = pl.ds(pl.multiple_of(i * tile, tile), tile)
            acc[:, at] += product(origin, c, at)

    last = half + 1

    @pl.loop(0, max(KVH, share_heads + last))
    def _(tick):
        def when(offset):
            c = tick - offset
            return c, pl.when((c >= 0) & (c < share_heads))

        for step in range(half + 1, 0, -1):
            c, guard = when(step)

            @guard
            def _(c=c, step=step):
                if step == 1:
                    for copy in own(c):
                        copy.wait()
                    for d in range(n_seq - 1):
                        across_in(c, d, 0).wait_recv()
                        across_in(c, d, 1).wait_recv()
                    for way in range(2):
                        ring_out(c, 1, way).start()
                    share(c, 0, 0, core).start()
                else:
                    for way in range(2):
                        ring_in(c, step - 1, way).wait_recv()
                        if step <= half:
                            ring_out(c, step, way).start()
                        share(c, step - 1, way, core).start()

        c, guard = when(0)

        @guard
        def _(c=c):
            for kind in range(2, 5):
                for d in range(n_seq - 1):
                    across_out(c, d, kind).start()

        @pl.when(tick < KVH)
        def _():
            weight(lax.rem(seq * share_heads + tick, KVH)).start()

        c, guard = when(last)

        @guard
        def _(c=c):
            for step, way in [(0, 0)] + hops:
                share(c, step, way, 1 - core).wait_recv()
            for d in range(n_seq - 1):
                for kind in range(2, 5):
                    across_in(c, d, kind).wait_recv()
            select(c)
            attend(c)

    project_own()

    @pl.loop(0, share_heads)
    def _(c):
        for d in range(n_seq - 1):
            for i in range(parts_per_head):
                attended(c, i, d, source(d), source(d)).wait_recv()
            project(source(d), c)

    out[0] = acc[...].astype(out.dtype)

    @pl.loop(0, share_heads)
    def _(c):
        for d in range(n_seq - 1):
            for kind in range(5):
                across_out(c, d, kind).wait_send()
            for i in range(parts_per_head):
                attended(c, i, d, seq, peers[d]).wait_send()
        for step, way in hops:
            ring_out(c, step, way).wait_send()
        for step, way in [(0, 0)] + hops:
            share(c, step, way, core).wait_send()


def per_device(n_leaf, n_seq, queries, leaf_kv, cache, out_weight, parent, owner, lengths):
    tokens = queries.shape[1]
    rows = cache.shape[0]
    cap = rows * n_seq
    total = tokens * n_seq
    cols = out_weight.shape[1]
    hops = n_leaf // 2
    heads = KVH // n_seq
    group = min(GROUP, 2 * max(1, 256 // total))
    parts = GROUP // group
    hbm = pl.BlockSpec(memory_space=pl.ANY)
    smem = pl.BlockSpec(memory_space=pltpu.SMEM)
    keys = DEPTH * cap + total
    dma = pltpu.SemaphoreType.DMA
    bf16 = jnp.bfloat16
    return pl.pallas_call(
        functools.partial(kernel, n_leaf, n_seq, cap),
        out_shape=jax.ShapeDtypeStruct((1, total, cols), bf16),
        in_specs=[hbm] * 4 + [smem] * 3,
        out_specs=pl.BlockSpec(memory_space=pltpu.VMEM),
        scratch_shapes=[
            pltpu.VMEM((heads, n_leaf, n_seq, 2, rows, HD), bf16),
            pltpu.VMEM((heads, n_seq, tokens, GROUP * HD), bf16),
            pltpu.VMEM((heads, n_seq, 2, tokens, HD), bf16),
            pltpu.VMEM((KVH, GROUP * HD, cols), bf16),
            pltpu.VMEM((keys, HD), bf16),
            pltpu.VMEM((keys, HD), bf16),
            pltpu.VMEM((n_seq, heads, parts, total, group * HD), bf16),
            pltpu.VMEM((total, cols), jnp.float32),
            pltpu.VMEM((8, DEPTH * cap), jnp.float32),
            dma((heads, 5)),
            dma((KVH,)),
            dma((heads, n_seq - 1, 5)),
            dma((heads, n_seq - 1, 5)),
            dma((heads, hops)),
            dma((heads, hops)),
            dma((heads, hops + 1)),
            dma((heads, hops + 1)),
            dma((heads, parts, n_seq - 1)),
            dma((heads, parts, n_seq - 1)),
        ],
        compiler_params=pltpu.CompilerParams(
            collective_id=0, has_side_effects=True, vmem_limit_bytes=58 * 1024 * 1024
        ),
    )(queries, leaf_kv, cache, out_weight, parent, owner, lengths)


def solution(mesh):
    in_specs = (
        P("leaf", "seq", None),
        P("leaf", "seq", None),
        P(("leaf", "seq"), None),
        P(None, "seq"),
        P(),
        P(),
        P(),
    )
    out_specs = P("leaf", None, "seq")
    return jax.shard_map(
        functools.partial(per_device, mesh.shape["leaf"], mesh.shape["seq"]),
        mesh=mesh, in_specs=in_specs, out_specs=out_specs, check_vma=False,
    )
```

```python
import functools
import math

import jax
import jax.numpy as jnp
from jax import lax
from jax.experimental import pallas as pl
from jax.experimental.pallas import tpu as pltpu
from jax.sharding import PartitionSpec as P

KVH = 8
GROUP = 8
HD = 128
DEPTH = 6
NEG = -1e30
MESH = pl.DeviceIdType.MESH


def kernel(
    n_leaf, n_seq, cap,
    q_hbm, leaf_hbm, cache_hbm, w_hbm, parent, owner, lengths,
    out,
    kvb, qb, lb, wb, kcat, vcat, att, acc, bias,
    local_sem, w_sem, y_send, y_recv, ring_send, ring_recv, sib_send, sib_recv,
    att_send, att_recv,
):
    chips = n_leaf // 2
    half = chips // 2
    tokens = q_hbm.shape[1]
    rows = cache_hbm.shape[0]
    all_tokens = n_seq * tokens
    cols = w_hbm.shape[1]
    me = lax.axis_index("leaf")
    seq = lax.axis_index("seq")
    core = lax.rem(me, 2)
    chip = me // 2
    side = lax.rem(chip, 2)
    level = chip // 2
    pos = level * (1 - side) + (chips - 1 - level) * side

    def slot_at(place, which):
        place = lax.rem(place + 2 * chips, chips)
        far = place // half
        return 2 * (2 * (place * (1 - far) + (chips - 1 - place) * far) + far) + which

    right = slot_at(pos + 1, core)
    left = slot_at(pos - 1, core)
    sibling = 2 * chip + 1 - core
    peers = [lax.rem(seq + d, n_seq) for d in range(1, n_seq)]

    share_heads = KVH // n_seq
    width = GROUP * HD

    def pieces(c, to):
        head = to * share_heads + c
        k_cols = pl.ds(pl.multiple_of(head * HD, HD), HD)
        v_cols = pl.ds(pl.multiple_of((KVH + head) * HD, HD), HD)
        q_cols = pl.ds(pl.multiple_of(head * width, width), width)
        return (
            cache_hbm.at[:, k_cols],
            cache_hbm.at[:, v_cols],
            leaf_hbm.at[0, :, k_cols],
            leaf_hbm.at[0, :, v_cols],
            q_hbm.at[0, :, q_cols],
        )

    def places(c, origin):
        return (
            kvb.at[c, me, origin, 0],
            kvb.at[c, me, origin, 1],
            lb.at[c, origin, 0],
            lb.at[c, origin, 1],
            qb.at[c, origin],
        )

    def own(c):
        return [
            pltpu.make_async_copy(src, dst, local_sem.at[c, i])
            for i, (src, dst) in enumerate(zip(pieces(c, seq), places(c, seq)))
        ]

    def weight(head):
        return pltpu.make_async_copy(
            w_hbm.at[pl.ds(pl.multiple_of(head * width, width), width), :],
            wb.at[head],
            w_sem.at[head],
        )

    def copy_to(src, dst, send, recv, leaf, s):
        return pltpu.make_async_remote_copy(
            src_ref=src, dst_ref=dst, send_sem=send, recv_sem=recv,
            device_id=(leaf, s), device_id_type=MESH,
        )

    def remote(ref, send, recv, leaf, s):
        return copy_to(ref, ref, send, recv, leaf, s)

    def source(d):
        return lax.rem(seq + n_seq - d - 1, n_seq)

    def across_out(c, d, kind):
        return copy_to(
            pieces(c, peers[d])[kind], places(c, seq)[kind],
            y_send.at[c, d, kind], y_recv.at[c, d, kind], me, peers[d],
        )

    def across_in(c, d, kind):
        ref = places(c, source(d))[kind]
        return remote(ref, y_send.at[c, d, kind], y_recv.at[c, d, kind], me, source(d))

    def attended(c, i, d, origin, to):
        ref = att.at[origin, c, i]
        return remote(ref, att_send.at[c, i, d], att_recv.at[c, i, d], me, to)

    def block(c, slot, step, way):
        if step < half:
            return kvb.at[c, slot]
        return kvb.at[c, slot, pl.ds(way * (n_seq // 2), n_seq // 2)]

    def ring_out(c, step, way):
        place = pos - (step - 1) if way == 0 else pos + (step - 1)
        ref = block(c, slot_at(place, core), step, way)
        i = 2 * (step - 1) + way
        return remote(ref, ring_send.at[c, i], ring_recv.at[c, i], (right, left)[way], seq)

    def ring_in(c, step, way):
        place = pos - step if way == 0 else pos + step
        ref = block(c, slot_at(place, core), step, way)
        i = 2 * (step - 1) + way
        return remote(ref, ring_send.at[c, i], ring_recv.at[c, i], (left, right)[way], seq)

    def share(c, step, way, which):
        place = pos - step if way == 0 else pos + step
        ref = block(c, slot_at(place, which), step, way)
        i = 0 if step == 0 else 1 + 2 * (step - 1) + way
        return remote(ref, sib_send.at[c, i], sib_recv.at[c, i], sibling, seq)

    hops = [(step, way) for step in range(1, half + 1) for way in range(2)]

    @pl.loop(0, share_heads)
    def _(c):
        for copy in own(c):
            copy.start()

    barrier = pltpu.get_barrier_semaphore()
    partners = [(right, seq), (left, seq), (sibling, seq)] + [(me, p) for p in peers]
    for partner in partners:
        pl.semaphore_signal(barrier, inc=1, device_id=partner, device_id_type=MESH)
    pl.semaphore_wait(barrier, len(partners))

    @pl.loop(0, share_heads)
    def _(c):
        for d in range(n_seq - 1):
            across_out(c, d, 0).start()
            across_out(c, d, 1).start()

    segment = parent[owner.shape[0] + me]
    slots = []
    for a in range(DEPTH):
        slots.append(owner[segment])
        lane = lax.broadcasted_iota(jnp.int32, (8, cap), 1)
        bias[:, a * cap:(a + 1) * cap] = jnp.where(lane < lengths[segment], 0.0, NEG)
        segment = parent[segment]

    stack = max(1, 256 // all_tokens)
    branch_keys = DEPTH * cap
    factor = math.log2(math.e) / math.sqrt(HD)

    def select(c):
        for j in range(n_seq):
            for part, cat in ((0, kcat), (1, vcat)):
                def pick(s, found):
                    piece = kvb[c, s, j, part]
                    return tuple(
                        lax.select(slots[a] == s, piece, found[a]) for a in range(DEPTH)
                    )
                zero = jnp.zeros((rows, HD), jnp.bfloat16)
                found = lax.fori_loop(0, n_leaf, pick, (zero,) * DEPTH, unroll=8)
                for a in range(DEPTH):
                    cat[a * cap + j * rows:a * cap + (j + 1) * rows, :] = found[a]
                at = branch_keys + j * tokens
                cat[at:at + tokens, :] = lb[c, j, part]

    def stacked(c, first):
        parts = []
        for g in range(stack):
            lanes = slice((first + g) * HD, (first + g + 1) * HD)
            for j in range(n_seq):
                parts.append(qb[c, j, :, lanes])
        q = jnp.concatenate(parts, axis=0)
        dims = (((1,), (1,)), ((), ()))
        scores = lax.dot_general(q, kcat[...], dims, preferred_element_type=jnp.float32)
        seen = scores[:, :branch_keys] + bias[0:1, :]
        count = stack * all_tokens
        row = lax.broadcasted_iota(jnp.int32, (count, all_tokens), 0)
        key = lax.broadcasted_iota(jnp.int32, (count, all_tokens), 1)
        own_keys = jnp.where(key <= lax.rem(row, all_tokens), scores[:, branch_keys:], NEG)
        scores = jnp.concatenate([seen, own_keys], axis=1)
        largest = jnp.max(scores, axis=1, keepdims=True)
        expon = jnp.exp2((scores - largest) * factor)
        total = jnp.sum(expon, axis=1, keepdims=True)
        summed = jnp.dot(
            expon.astype(jnp.bfloat16), vcat[...], preferred_element_type=jnp.float32
        )
        result = (summed / total).astype(jnp.bfloat16)
        return [result[g * all_tokens:(g + 1) * all_tokens] for g in range(stack)]

    parts_per_head = att.shape[2]
    group = GROUP // parts_per_head

    def attend(c):
        for i in range(parts_per_head):
            results = []
            for first in range(0, group, stack):
                results += stacked(c, i * group + first)
            att[seq, c, i] = jnp.concatenate(results, axis=1)
            for d in range(n_seq - 1):
                attended(c, i, d, seq, peers[d]).start()

    tile = math.gcd(cols, 512)

    def rows_of(origin, c):
        return jnp.concatenate([att[origin, c, i] for i in range(parts_per_head)], axis=1)

    def product(origin, c, at):
        head = origin * share_heads + c
        return jnp.dot(rows_of(origin, c), wb[head, :, at], preferred_element_type=jnp.float32)

    def project_own():
        for c in range(share_heads):
            weight(seq * share_heads + c).wait()

        @pl.loop(0, cols // tile)
        def _(i):
            at = pl.ds(pl.multiple_of(i * tile, tile), tile)
            part = product(seq, 0, at)
            for c in range(1, share_heads):
                part += product(seq, c, at)
            acc[:, at] = part

    def project(origin, c):
        weight(origin * share_heads + c).wait()

        @pl.loop(0, cols // tile)
        def _(i):
            at = pl.ds(pl.multiple_of(i * tile, tile), tile)
            acc[:, at] += product(origin, c, at)

    last = half + 1

    @pl.loop(0, max(KVH, share_heads + last))
    def _(tick):
        def when(offset):
            c = tick - offset
            return c, pl.when((c >= 0) & (c < share_heads))

        for step in range(half + 1, 0, -1):
            c, guard = when(step)

            @guard
            def _(c=c, step=step):
                if step == 1:
                    for copy in own(c):
                        copy.wait()
                    for d in range(n_seq - 1):
                        across_in(c, d, 0).wait_recv()
                        across_in(c, d, 1).wait_recv()
                    for way in range(2):
                        ring_out(c, 1, way).start()
                    share(c, 0, 0, core).start()
                else:
                    for way in range(2):
                        ring_in(c, step - 1, way).wait_recv()
                        if step <= half:
                            ring_out(c, step, way).start()
                        share(c, step - 1, way, core).start()

        c, guard = when(0)

        @guard
        def _(c=c):
            for kind in range(2, 5):
                for d in range(n_seq - 1):
                    across_out(c, d, kind).start()

        @pl.when(tick < KVH)
        def _():
            weight(lax.rem(seq * share_heads + tick, KVH)).start()

        c, guard = when(last)

        @guard
        def _(c=c):
            for step, way in [(0, 0)] + hops:
                share(c, step, way, 1 - core).wait_recv()
            for d in range(n_seq - 1):
                for kind in range(2, 5):
                    across_in(c, d, kind).wait_recv()
            select(c)
            attend(c)

    project_own()

    @pl.loop(0, share_heads)
    def _(c):
        for d in range(n_seq - 1):
            for i in range(parts_per_head):
                attended(c, i, d, source(d), source(d)).wait_recv()
            project(source(d), c)

    out[0] = acc[...].astype(out.dtype)

    @pl.loop(0, share_heads)
    def _(c):
        for d in range(n_seq - 1):
            for kind in range(5):
                across_out(c, d, kind).wait_send()
            for i in range(parts_per_head):
                attended(c, i, d, seq, peers[d]).wait_send()
        for step, way in hops:
            ring_out(c, step, way).wait_send()
        for step, way in [(0, 0)] + hops:
            share(c, step, way, core).wait_send()


def per_device(n_leaf, n_seq, queries, leaf_kv, cache, out_weight, parent, owner, lengths):
    tokens = queries.shape[1]
    rows = cache.shape[0]
    cap = rows * n_seq
    total = tokens * n_seq
    cols = out_weight.shape[1]
    hops = n_leaf // 2
    heads = KVH // n_seq
    group = min(GROUP, 2 * max(1, 256 // total))
    parts = GROUP // group
    hbm = pl.BlockSpec(memory_space=pl.ANY)
    smem = pl.BlockSpec(memory_space=pltpu.SMEM)
    keys = DEPTH * cap + total
    dma = pltpu.SemaphoreType.DMA
    bf16 = jnp.bfloat16
    return pl.pallas_call(
        functools.partial(kernel, n_leaf, n_seq, cap),
        out_shape=jax.ShapeDtypeStruct((1, total, cols), bf16),
        in_specs=[hbm] * 4 + [smem] * 3,
        out_specs=pl.BlockSpec(memory_space=pltpu.VMEM),
        scratch_shapes=[
            pltpu.VMEM((heads, n_leaf, n_seq, 2, rows, HD), bf16),
            pltpu.VMEM((heads, n_seq, tokens, GROUP * HD), bf16),
            pltpu.VMEM((heads, n_seq, 2, tokens, HD), bf16),
            pltpu.VMEM((KVH, GROUP * HD, cols), bf16),
            pltpu.VMEM((keys, HD), bf16),
            pltpu.VMEM((keys, HD), bf16),
            pltpu.VMEM((n_seq, heads, parts, total, group * HD), bf16),
            pltpu.VMEM((total, cols), jnp.float32),
            pltpu.VMEM((8, DEPTH * cap), jnp.float32),
            dma((heads, 5)),
            dma((KVH,)),
            dma((heads, n_seq - 1, 5)),
            dma((heads, n_seq - 1, 5)),
            dma((heads, hops)),
            dma((heads, hops)),
            dma((heads, hops + 1)),
            dma((heads, hops + 1)),
            dma((heads, parts, n_seq - 1)),
            dma((heads, parts, n_seq - 1)),
        ],
        compiler_params=pltpu.CompilerParams(
            collective_id=0, has_side_effects=True, vmem_limit_bytes=58 * 1024 * 1024
        ),
    )(queries, leaf_kv, cache, out_weight, parent, owner, lengths)


def solution(mesh):
    in_specs = (
        P("leaf", "seq", None),
        P("leaf", "seq", None),
        P(("leaf", "seq"), None),
        P(None, "seq"),
        P(),
        P(),
        P(),
    )
    out_specs = P("leaf", None, "seq")
    return jax.shard_map(
        functools.partial(per_device, mesh.shape["leaf"], mesh.shape["seq"]),
        mesh=mesh, in_specs=in_specs, out_specs=out_specs, check_vma=False,
    )
```
